512 devices in a mesh: leaf: 64 (over z, x), front: 8 (over y, core).
Axes of the slice: x: 4, y: 4, z: 16, core: 2. Of those that a mesh axis runs over, the one named last changes fastest.
Arguments:
- fields: bfloat16 [2, 48, 65536], P(None, None, ('leaf', 'front')), may hold values from -6 to 6
- direction: float32 [2, 65536], P(None, ('leaf', 'front')), may hold values from -6 to 6
- inverse_blocks: bfloat16 [2, 65536, 1024], P(None, ('leaf', 'front')), may hold values from -1.5 to 1.5
- update_blocks: bfloat16 [2, 65536, 1024], P(None, ('leaf', 'front')), may hold values from -0.125 to 0.125
- row_map: int32 [2, 64, 1024], P(None, 'leaf'), may hold values from 0 to 1023, each once within a row
- receivers: int32 [64, 128], P('leaf'), may hold values from 0 to 1023
- weights: float32 [64, 128], P('leaf'), may hold values from 0.05 to 0.5
Outputs:
- data_change: bfloat16 [48, 8192], P(None, 'leaf')
- curvature: float32 [2, 65536], P(None, ('leaf', 'front'))
The draws below stay inside these ranges and needn't reach their ends.
Inputs may be any that keep to these rules, and one draw needn't show every extreme that they name: Each row_map[k, g] is a permutation of 0 .. 1023.
All inputs are finite; a program needn't handle non-finite values.
Results may differ from the reference program's by a relative error of at most 0.033.
Values may be sent and summed in bfloat16 or wider, within the bound.
No kernel may reach another device: no remote copies, remote signals or barrier semaphores. Data moves between devices by JAX's collectives and lax.ppermute only.
A program may use at most 64 MiB of HBM per device.

```python
import math
import jax
import jax.numpy as jnp
import numpy as np
from jax import lax

FRONT_ROWS = 1024
SOURCES = 48
STATIONS = 128
GROUPS = 64
LEVELS = 6
ALL_ROWS = 65536
N_FRONT = 8


def draw_inverse_blocks(key, part):
    key = jax.random.fold_in(key, 17)
    noise_key, diag_key = jax.random.split(key)
    row_pos = jnp.arange(ALL_ROWS) % FRONT_ROWS
    col_pos = jnp.arange(FRONT_ROWS)
    below_diag = (col_pos[None, :] < row_pos[:, None]).astype(jnp.float32)
    on_diag = (col_pos[None, :] == row_pos[:, None]).astype(jnp.float32)
    full_shape = (2, ALL_ROWS, FRONT_ROWS)
    noise_vals = jax.random.normal(noise_key, full_shape, jnp.float32)
    diagonal = jax.random.uniform(diag_key, (2, ALL_ROWS, 1), jnp.float32, 0.7, 1.3)
    lower_part = below_diag[None, :, :] * noise_vals * (0.5 / math.sqrt(FRONT_ROWS))
    return (lower_part + on_diag[None, :, :] * diagonal).astype(jnp.bfloat16)


def plant(values, stream_key, smallest, largest):
    dims = values.shape
    place = [jax.random.randint(jax.random.fold_in(stream_key, axis), (), 0, dims[axis]) for axis in range(len(dims))]
    values = values.at[tuple(place)].set(smallest)
    longest = dims.index(max(dims))
    place[longest] = (place[longest] + 1) % dims[longest]
    return values.at[tuple(place)].set(largest)


def block_scale(key, extent, shards, low, largest):
    factor_of = 1.0
    for position, shards_of in shards:
        heights = jax.random.uniform(jax.random.fold_in(jax.random.fold_in(key, 6), position), (shards_of,), jnp.float32, low / len(shards), largest / len(shards))
        factor_of = factor_of * jnp.repeat(jnp.exp(heights), extent[position] // shards_of).reshape((-1,) + (1,) * (len(extent) - 1 - position))
    return factor_of


def noise(key, extent, scale, limit, pieces=(), kind=jnp.bfloat16):
    level = block_scale(key, extent, pieces, -0.22, 0.18) if pieces else 1.0
    result = jax.random.normal(key, extent, jnp.float32) * scale * level
    return jnp.minimum(jnp.maximum(result, -limit), limit).astype(kind)


def setup_inputs(seed: int = 0) -> dict:
    splits = jax.random.split(jax.random.key(seed), 8)
    return {
        "fields": noise(splits[0], (2, SOURCES, ALL_ROWS), 1.0, 6.0, ((2, 512),)),
        "direction": noise(splits[1], (2, ALL_ROWS), 1.0, 6.0, ((1, 512),), jnp.float32),
        "inverse_blocks": draw_inverse_blocks(jax.random.fold_in(splits[7], 71), 0),
        "update_blocks": noise(splits[3], (2, ALL_ROWS, FRONT_ROWS), (2 * FRONT_ROWS) ** -0.5, 0.125, ((1, 512),)),
        "row_map": jax.vmap(lambda own: jax.random.permutation(own, FRONT_ROWS))(jax.random.split(splits[4], 2 * GROUPS)).reshape((2, GROUPS, FRONT_ROWS)).astype(jnp.int32),
        "receivers": plant(jax.random.randint(splits[5], (GROUPS, STATIONS), 0, FRONT_ROWS), jax.random.fold_in(splits[5], 1), 0, FRONT_ROWS - 1).astype(jnp.int32),
        "weights": jnp.clip(jnp.exp(math.log(0.5) - 2.3025851 * jax.random.uniform(splits[6], (GROUPS, STATIONS), jnp.float32) ** block_scale(splits[6], (GROUPS, STATIONS), ((0, 64),), -0.2, 0.2)), 0.05, 0.5),
    }


def owners_at(height):
    return np.arange(GROUPS >> height) * (2 ** height) + 2 ** (height - 1)


def apply_front(vectors, matrix):
    return jnp.einsum('csj,cij->csi', vectors.astype(jnp.float32), matrix.astype(jnp.float32)).astype(jnp.bfloat16)


def add_columns(base, columns, values):
    return base.at[:, columns].add(values)


def take_columns(values, columns):
    return jnp.take(values, columns, axis=1)


def back_front(solved, parent_vals, inverse_mat, update_mat):
    group_count = solved.shape[0]
    block_rows = FRONT_ROWS // N_FRONT
    solved_blocks = solved.astype(jnp.float32).reshape(group_count, SOURCES, N_FRONT, block_rows)
    parent_blocks = parent_vals.astype(jnp.float32).reshape(group_count, SOURCES, N_FRONT, block_rows)
    inverse_split = inverse_mat.astype(jnp.float32).reshape(group_count, N_FRONT, block_rows, FRONT_ROWS)
    update_split = update_mat.astype(jnp.float32).reshape(group_count, N_FRONT, block_rows, FRONT_ROWS)
    terms = jnp.einsum('cski,ckiw->cksw', solved_blocks, inverse_split)
    terms = terms - jnp.einsum('cski,ckiw->cksw', parent_blocks, update_split)
    rounded = lax.optimization_barrier(terms.astype(jnp.bfloat16))
    return jnp.sum(rounded.astype(jnp.float32), axis=1).astype(jnp.bfloat16)


def solve(leaf_source, node_source, inverse_all, update_all, row_map):
    leaf_solved = apply_front(leaf_source, inverse_all[0])
    leaf_update = apply_front(leaf_source, update_all[0])
    node_solved = jnp.zeros_like(leaf_solved)
    node_update = jnp.zeros_like(leaf_solved)
    for height in range(1, LEVELS + 1):
        owners = owners_at(height)
        if height == 1:
            left_update = leaf_update[owners - 1]
            left_map = row_map[0][owners - 1]
            right_update = leaf_update[owners]
            right_map = row_map[0][owners]
        else:
            offset = 2 ** (height - 2)
            left_update = node_update[owners - offset]
            left_map = row_map[1][owners - offset]
            right_update = node_update[owners + offset]
            right_map = row_map[1][owners + offset]
        residual = node_source[owners].astype(jnp.float32)
        residual = jax.vmap(add_columns)(residual, left_map, -left_update.astype(jnp.float32))
        residual = jax.vmap(add_columns)(residual, right_map, -right_update.astype(jnp.float32))
        residual = residual.astype(jnp.bfloat16)
        node_solved = node_solved.at[owners].set(apply_front(residual, inverse_all[1][owners]))
        node_update = node_update.at[owners].set(apply_front(residual, update_all[1][owners]))
    node_whole = jnp.zeros_like(leaf_solved)
    for height in range(LEVELS, 0, -1):
        owners = owners_at(height)
        if height == LEVELS:
            parent_vals = jnp.zeros((owners.shape[0], SOURCES, FRONT_ROWS), jnp.bfloat16)
        else:
            on_left = (owners // (2 ** height)) % 2 == 0
            parents = np.where(on_left, owners + 2 ** (height - 1), owners - 2 ** (height - 1))
            parent_vals = jax.vmap(take_columns)(node_whole[parents], row_map[1][owners])
        node_whole = node_whole.at[owners].set(back_front(node_solved[owners], parent_vals, inverse_all[1][owners], update_all[1][owners]))
    leaf_parents = np.arange(GROUPS) | 1
    leaf_parent_vals = jax.vmap(take_columns)(node_whole[leaf_parents], row_map[0])
    leaf_whole = back_front(leaf_solved, leaf_parent_vals, inverse_all[0], update_all[0])
    return leaf_whole, node_whole


def inject(station_vals, station_rows, station_weights):
    base = jnp.zeros((SOURCES, FRONT_ROWS), jnp.float32)
    added = base.at[:, station_rows].add(station_weights[None, :] * station_vals.astype(jnp.float32))
    return added.astype(jnp.bfloat16)


def reference(fields, direction, inverse_blocks, update_blocks, row_map, receivers, weights):
    field_groups = fields.reshape(2, SOURCES, GROUPS, FRONT_ROWS).transpose(0, 2, 1, 3)
    direction_groups = direction.reshape(2, GROUPS, FRONT_ROWS)
    source_terms = (direction_groups[:, :, None, :] * field_groups.astype(jnp.float32)).astype(jnp.bfloat16)
    inverse_all = inverse_blocks.reshape(2, GROUPS, FRONT_ROWS, FRONT_ROWS)
    update_all = update_blocks.reshape(2, GROUPS, FRONT_ROWS, FRONT_ROWS)
    delta_leaf, delta_node = solve(source_terms[0], source_terms[1], inverse_all, update_all, row_map)
    station_vals = jax.vmap(take_columns)(delta_leaf, receivers)
    data_change = station_vals.transpose(1, 0, 2).reshape(SOURCES, GROUPS * STATIONS)
    adjoint_leaf_terms = jax.vmap(inject)(station_vals, receivers, weights)
    adjoint_node_terms = jnp.zeros_like(adjoint_leaf_terms)
    adjoint_leaf, adjoint_node = solve(adjoint_leaf_terms, adjoint_node_terms, inverse_all, update_all, row_map)
    curve_leaf = jnp.sum(field_groups[0].astype(jnp.float32) * adjoint_leaf.astype(jnp.float32), axis=1)
    curve_node = jnp.sum(field_groups[1].astype(jnp.float32) * adjoint_node.astype(jnp.float32), axis=1)
    curvature = jnp.stack([curve_leaf.reshape(GROUPS * FRONT_ROWS), curve_node.reshape(GROUPS * FRONT_ROWS)])
    return data_change, curvature
```

```python
import jax
import jax.numpy as jnp
from jax import lax
from jax.sharding import PartitionSpec as P

CONTRACT_LAST = (((1,), (1,)), ((), ()))


def times_transposed(vectors, matrix):
    return lax.dot_general(vectors, matrix, CONTRACT_LAST, preferred_element_type=jnp.float32)


def times(vectors, matrix):
    return jnp.dot(vectors, matrix, preferred_element_type=jnp.float32)


def owners_at(height, groups):
    return [g for g in range(1, groups) if (g & -g) == 1 << (height - 1)]


def links(height, groups):
    owners = owners_at(height, groups)
    if height == 1:
        return [(g - 1, g) for g in owners], []
    offset = 2 ** (height - 2)
    return [(g - offset, g) for g in owners], [(g + offset, g) for g in owners]


def send(value, pairs):
    return lax.ppermute(value, "leaf", pairs)


def reverse(pairs):
    return [(b, a) for a, b in pairs]


def forward(leaf_r, node_r, leaf_up, node_up, is_first, levels, groups):
    update = times_transposed(leaf_r, leaf_up).astype(jnp.bfloat16)
    node_r = node_r.astype(jnp.float32)
    for height in range(1, levels + 1):
        left, right = links(height, groups)
        from_left = send(update, left).astype(jnp.float32)
        if height == 1:
            from_right = jnp.where(is_first, update.astype(jnp.float32), 0.0)
        else:
            from_right = send(update, right).astype(jnp.float32)
        node_r = node_r - from_left - from_right
        if height < levels:
            update = times_transposed(node_r.astype(jnp.bfloat16), node_up).astype(jnp.bfloat16)
    return node_r.astype(jnp.bfloat16)


def backward(leaf_t, node_t, leaf_up, node_up, is_first, levels, groups):
    node_x = node_t.astype(jnp.bfloat16)
    for height in range(levels, 1, -1):
        left, right = links(height, groups)
        z = send(node_x, reverse(left)) + send(node_x, reverse(right))
        new_x = (node_t - times(z, node_up)).astype(jnp.bfloat16)
        group = lax.axis_index("leaf")
        mine = (group & -group) == 1 << (height - 2)
        node_x = jnp.where(mine, new_x, node_x)
    left, _ = links(1, groups)
    z = jnp.where(is_first, node_x, send(node_x, reverse(left)))
    leaf_x = (leaf_t - times(z, leaf_up)).astype(jnp.bfloat16)
    return leaf_x, node_x


def solve(leaf_r, node_r, mats, is_first, levels, groups):
    leaf_up, node_up, leaf_inv, node_inv = mats
    node_r = forward(leaf_r, node_r, leaf_up, node_up, is_first, levels, groups)
    leaf_t = times(times_transposed(leaf_r, leaf_inv).astype(jnp.bfloat16), leaf_inv)
    node_t = times(times_transposed(node_r, node_inv).astype(jnp.bfloat16), node_inv)
    return backward(leaf_t, node_t, leaf_up, node_up, is_first, levels, groups)


def per_device(fields, direction, inverse_blocks, update_blocks, row_map, receivers, weights):
    groups = lax.axis_size("leaf")
    width = lax.axis_size("front")
    levels = groups.bit_length() - 1
    is_first = lax.axis_index("leaf") % 2 == 1
    sources, rows = fields.shape[1], fields.shape[2]
    share = sources // width
    whole = rows * width

    terms = (direction[:, None, :] * fields.astype(jnp.float32)).astype(jnp.bfloat16)
    packed = jnp.concatenate([fields, terms], 0).reshape(4, width, share, rows).transpose(1, 0, 2, 3)
    packed = lax.all_to_all(packed, "front", 0, 0, tiled=True)
    packed = packed.transpose(1, 2, 0, 3).reshape(4, share, whole)
    field_leaf, field_node, term_leaf, term_node = packed[0], packed[1], packed[2], packed[3]

    def gather(block):
        return lax.all_gather(block, "front", axis=0, tiled=True)

    def placed(matrix, columns):
        spots = (jnp.arange(whole)[:, None] == columns[None, :]).astype(jnp.bfloat16)
        return times(spots, matrix).astype(jnp.bfloat16)

    leaf_up = placed(gather(update_blocks[0]), row_map[0, 0])
    node_up = placed(gather(update_blocks[1]), row_map[1, 0])
    leaf_inv = gather(inverse_blocks[0])
    node_inv = gather(inverse_blocks[1])
    mats = (leaf_up, node_up, leaf_inv, node_inv)

    at_station = receivers[0][:, None] == jnp.arange(whole)[None, :]
    station_weight = jnp.sum(jnp.where(at_station, weights[0][:, None], 0.0), axis=0)

    delta_leaf, _ = solve(term_leaf, term_node, mats, is_first, levels, groups)
    injected = (delta_leaf.astype(jnp.float32) * station_weight[None, :]).astype(jnp.bfloat16)
    station = times_transposed(delta_leaf, at_station.astype(jnp.bfloat16))
    adj_leaf, adj_node = solve(injected, jnp.zeros_like(term_node), mats, is_first, levels, groups)
    curve_leaf = jnp.sum(field_leaf.astype(jnp.float32) * adj_leaf.astype(jnp.float32), axis=0)
    curve_node = jnp.sum(field_node.astype(jnp.float32) * adj_node.astype(jnp.float32), axis=0)

    curve = jnp.stack([curve_leaf, curve_node]).reshape(2, width, rows).transpose(1, 0, 2)
    out = jnp.concatenate([curve, jnp.broadcast_to(station[None], (width,) + station.shape)], axis=1)
    out = lax.all_to_all(out, "front", 0, 0, tiled=True)
    curvature = jnp.sum(out[:, :2], axis=0)
    data_change = out[:, 2:].reshape(sources, station.shape[1]).astype(jnp.bfloat16)
    return data_change, curvature


def solution(mesh):
    in_specs = (
        P(None, None, ("leaf", "front")),
        P(None, ("leaf", "front")),
        P(None, ("leaf", "front"), None),
        P(None, ("leaf", "front"), None),
        P(None, "leaf", None),
        P("leaf", None),
        P("leaf", None),
    )
    out_specs = (P(None, "leaf"), P(None, ("leaf", "front")))
    return jax.shard_map(
        per_device, mesh=mesh, in_specs=in_specs, out_specs=out_specs, check_vma=False
    )
```

```python
import jax
import jax.numpy as jnp
from jax import lax
from jax.sharding import PartitionSpec as P

CONTRACT_LAST = (((1,), (1,)), ((), ()))


def times_transposed(vectors, matrix):
    return lax.dot_general(vectors, matrix, CONTRACT_LAST, preferred_element_type=jnp.float32)


def times(vectors, matrix):
    return jnp.dot(vectors, matrix, preferred_element_type=jnp.float32)


def owners_at(height, groups):
    return [g for g in range(1, groups) if (g & -g) == 1 << (height - 1)]


def links(height, groups):
    owners = owners_at(height, groups)
    if height == 1:
        return [(g - 1, g) for g in owners], []
    offset = 2 ** (height - 2)
    return [(g - offset, g) for g in owners], [(g + offset, g) for g in owners]


def send(value, pairs):
    return lax.ppermute(value, "leaf", pairs)


def reverse(pairs):
    return [(b, a) for a, b in pairs]


def forward(update, node_r, node_up, is_first, levels, groups):
    node_r = node_r.astype(jnp.float32)
    for height in range(1, levels + 1):
        left, right = links(height, groups)
        from_left = send(update, left).astype(jnp.float32)
        if height == 1:
            from_right = jnp.where(is_first, update.astype(jnp.float32), 0.0)
        else:
            from_right = send(update, right).astype(jnp.float32)
        node_r = node_r - from_left - from_right
        if height < levels:
            update = times_transposed(node_r.astype(jnp.bfloat16), node_up).astype(jnp.bfloat16)
    return node_r.astype(jnp.bfloat16)


def backward(leaf_t, node_t, leaf_up, node_up, is_first, levels, groups):
    node_x = node_t.astype(jnp.bfloat16)
    for height in range(levels, 1, -1):
        left, right = links(height, groups)
        z = send(node_x, reverse(left)) + send(node_x, reverse(right))
        new_x = (node_t - times(z, node_up)).astype(jnp.bfloat16)
        group = lax.axis_index("leaf")
        mine = (group & -group) == 1 << (height - 2)
        node_x = jnp.where(mine, new_x, node_x)
    left, _ = links(1, groups)
    z = jnp.where(is_first, node_x, send(node_x, reverse(left)))
    leaf_x = (leaf_t - times(z, leaf_up)).astype(jnp.bfloat16)
    return leaf_x, node_x


def gather_rows(block):
    count = lax.axis_size("front")

    def shifted(by):
        return lax.ppermute(block, "front", [(f, (f + by) % count) for f in range(count)])

    near = [block, shifted(2), shifted(-2), shifted(4)] if count == 8 else [block]
    near = jnp.concatenate(near, 0)
    far = lax.ppermute(near, "front", [(f, f ^ 1) for f in range(count)])
    return jnp.concatenate([near, far], 0)


def gathered_order(columns):
    count = lax.axis_size("front")
    here = lax.axis_index("front")
    steps = jnp.array([0, -2, 2, 4] if count == 8 else [0])
    near = (here + steps) % count
    order = jnp.concatenate([near, near ^ 1])
    return columns.reshape(count, -1)[order].reshape(-1)


def per_device(fields, direction, inverse_blocks, update_blocks, row_map, receivers, weights):
    groups = lax.axis_size("leaf")
    width = lax.axis_size("front")
    levels = groups.bit_length() - 1
    is_first = lax.axis_index("leaf") % 2 == 1
    sources, rows = fields.shape[1], fields.shape[2]
    share = sources // width
    whole = rows * width

    def own(axis_rows):
        return axis_rows.transpose(1, 0, 2).reshape(axis_rows.shape[1], whole)

    terms = (direction[:, None, :] * fields.astype(jnp.float32)).astype(jnp.bfloat16)
    packed = jnp.concatenate([fields, terms], 0).reshape(4, width, share, rows).transpose(1, 0, 2, 3)
    packed = packed.reshape(width, 4 * share, rows)
    packed = jnp.concatenate([packed, jnp.broadcast_to(terms[:1], (width, sources, rows))], 1)
    packed = lax.all_to_all(packed, "front", 0, 0, tiled=True)
    leaf_all = own(packed[:, 4 * share :])
    field_leaf, field_node, term_leaf, term_node = [
        own(packed[:, k * share : (k + 1) * share]) for k in range(4)
    ]

    node_rows = gather_rows(update_blocks[1])
    later = jnp.stack([inverse_blocks[1], inverse_blocks[0], update_blocks[0]])
    later = lax.all_gather(later, "front", axis=0)

    def spots(columns):
        return (jnp.arange(whole)[:, None] == columns[None, :]).astype(jnp.bfloat16)

    def squared(blocks):
        return lax.dot_general(
            blocks, blocks, (((0, 1), (0, 1)), ((), ())), preferred_element_type=jnp.float32
        ).astype(jnp.bfloat16)

    leaf_spots = spots(row_map[0, 0])
    node_up = times(spots(gathered_order(row_map[1, 0])), node_rows).astype(jnp.bfloat16)

    at_station = receivers[0][:, None] == jnp.arange(whole)[None, :]
    station_weight = jnp.sum(jnp.where(at_station, weights[0][:, None], 0.0), axis=0)

    update = times_transposed(leaf_all, update_blocks[0]).astype(jnp.bfloat16)
    update = lax.all_to_all(update.reshape(width, share, rows), "front", 0, 0, tiled=True)
    update = times_transposed(own(update), leaf_spots).astype(jnp.bfloat16)
    node_r = forward(update, term_node, node_up, is_first, levels, groups)
    node_inv = squared(later[:, 0])
    leaf_inv = squared(later[:, 1])
    leaf_up = times(leaf_spots, later[:, 2].reshape(whole, whole)).astype(jnp.bfloat16)
    node_t = times(node_r, node_inv)
    leaf_t = times(term_leaf, leaf_inv)
    delta_leaf, _ = backward(leaf_t, node_t, leaf_up, node_up, is_first, levels, groups)
    injected = (delta_leaf.astype(jnp.float32) * station_weight[None, :]).astype(jnp.bfloat16)
    station = times_transposed(delta_leaf, at_station.astype(jnp.bfloat16))

    update = times_transposed(injected, leaf_up).astype(jnp.bfloat16)
    node_r = forward(update, jnp.zeros_like(term_node), node_up, is_first, levels, groups)
    node_t = times(node_r, node_inv)
    leaf_t = times(injected, leaf_inv)
    adj_leaf, adj_node = backward(leaf_t, node_t, leaf_up, node_up, is_first, levels, groups)
    curve_leaf = jnp.sum(field_leaf.astype(jnp.float32) * adj_leaf.astype(jnp.float32), axis=0)
    curve_node = jnp.sum(field_node.astype(jnp.float32) * adj_node.astype(jnp.float32), axis=0)

    curve = jnp.stack([curve_leaf, curve_node]).reshape(2, width, rows).transpose(1, 0, 2)
    out = jnp.concatenate([curve, jnp.broadcast_to(station[None], (width,) + station.shape)], axis=1)
    out = lax.all_to_all(out, "front", 0, 0, tiled=True)
    curvature = jnp.sum(out[:, :2], axis=0)
    data_change = out[:, 2:].reshape(sources, station.shape[1]).astype(jnp.bfloat16)
    return data_change, curvature


def solution(mesh):
    in_specs = (
        P(None, None, ("leaf", "front")),
        P(None, ("leaf", "front")),
        P(None, ("leaf", "front"), None),
        P(None, ("leaf", "front"), None),
        P(None, "leaf", None),
        P("leaf", None),
        P("leaf", None),
    )
    out_specs = (P(None, "leaf"), P(None, ("leaf", "front")))
    return jax.shard_map(
        per_device, mesh=mesh, in_specs=in_specs, out_specs=out_specs, check_vma=False
    )
```

```python
import jax
import jax.numpy as jnp
from jax import lax
from jax.sharding import Mesh, PartitionSpec as P

LEAF = ("pair", "side")
FRONT = ("y", "core")
PAIR = ("side",) + FRONT
CONTRACT_LAST = (((1,), (1,)), ((), ()))
CONTRACT_FIRST = (((0,), (0,)), ((), ()))
PAD = 8


def times_transposed(vectors, matrix):
    return lax.dot_general(vectors, matrix, CONTRACT_LAST, preferred_element_type=jnp.float32)


def times(vectors, matrix):
    return jnp.dot(vectors, matrix, preferred_element_type=jnp.float32)


def rounded(values):
    return values.astype(jnp.bfloat16)


def after(value, *earlier):
    return lax.optimization_barrier((value,) + earlier)[0]


def links(height, groups):
    owners = [g for g in range(1, groups) if (g & -g) == 1 << (height - 1)]
    offset = 2 ** (height - 2)
    return [(g - offset, g) for g in owners], [(g + offset, g) for g in owners]


def reverse(pairs):
    return [(b, a) for a, b in pairs]


def send(value, pairs):
    return lax.ppermute(value, LEAF, pairs)


def y_blocks(block):
    count = lax.axis_size("y")

    def shifted(by):
        return lax.ppermute(block, "y", [(k, (k + by) % count) for k in range(count)])

    return [shifted(1), block, shifted(-1), shifted(2)]


def stacked(blocks):
    return jnp.concatenate(blocks, -2)


def core_swap(value):
    return lax.ppermute(value, "core", [(0, 1), (1, 0)])


def near_order(columns):
    count = lax.axis_size("y")
    blocks = columns.reshape(count, 2, -1)
    blocks = jnp.concatenate([blocks, blocks], 0)
    start = (lax.axis_index("y") + count - 1) % count
    blocks = lax.dynamic_slice_in_dim(blocks, start, count, 0)
    first, second = blocks[:, 0].reshape(-1), blocks[:, 1].reshape(-1)
    on_first = lax.axis_index("core") == 0
    return jnp.where(on_first, first, second), jnp.where(on_first, second, first)


def per_device(fields, direction, inverse_blocks, update_blocks, row_map, receivers, weights):
    groups = lax.axis_size(LEAF)
    width = lax.axis_size(FRONT)
    levels = groups.bit_length() - 1
    group = lax.axis_index(LEAF)
    odd = lax.axis_index("side") == 1
    sources, rows = fields.shape[1], fields.shape[2]
    share = sources // width
    whole = rows * width
    pair_up = [(g, g + 1) for g in range(0, groups, 2)]

    def lanes(blocks):
        blocks = blocks.reshape((-1,) + blocks.shape[-2:])
        return blocks.transpose(1, 0, 2).reshape(blocks.shape[1], -1)

    def padded(values):
        return jnp.pad(values.reshape(width, share, rows), ((0, 0), (0, PAD - share), (0, 0)))

    terms = rounded(direction[:, None, :] * fields.astype(jnp.float32))
    leaf_terms = padded(terms[0])
    map_rows = lax.dynamic_slice_in_dim(row_map[0, 0], lax.axis_index(FRONT) * rows, rows)
    digits = jnp.stack([map_rows // 32, map_rows % 32]).astype(jnp.bfloat16)
    digits = jnp.broadcast_to(digits[None], (width, 2, rows))

    def marked(values):
        return jnp.concatenate([values.reshape(width, share, rows), digits], 1)

    own = jnp.broadcast_to(leaf_terms.reshape(1, width * PAD, rows), (width, width * PAD, rows))
    own = jnp.concatenate([padded(fields[1]), padded(terms[1]), own], 1)
    message = jnp.concatenate(
        [jnp.concatenate([marked(terms[0]), own], 1), jnp.concatenate([marked(fields[0]), own], 1)], 0
    )
    node_block = update_blocks[1]
    swapped = after(jnp.where(odd, inverse_blocks[0], update_blocks[0]), message)
    message = lax.all_to_all(message, PAIR, 0, 0, tiled=True)
    message = message.reshape((2, width) + message.shape[1:])
    leaf_pair = lanes(message[:, :, :PAD])
    pair_map = leaf_pair[share].astype(jnp.float32) * 32 + leaf_pair[share + 1].astype(jnp.float32)
    pair_map = pair_map.astype(jnp.int32)
    mine = jnp.where(odd, message[1], message[0])
    field_node = lanes(mine[:, PAD : 2 * PAD])
    term_node = lanes(mine[:, 2 * PAD : 3 * PAD])
    leaf_all = lanes(mine[:, 3 * PAD :])

    def spots(columns):
        return (jnp.arange(whole)[:, None] == columns[None, :]).astype(jnp.bfloat16)

    node_near = stacked(y_blocks(node_block))
    node_far = core_swap(node_near)
    kept = jnp.where(odd, update_blocks[0], inverse_blocks[0])
    swapped = send(swapped, pair_up + reverse(pair_up))
    arrived = message[0, 0, 0, 0]
    held = node_near[0, 0] + node_near[2 * rows, 0] + node_near[3 * rows, 0]
    on_odd = odd ^ (arrived != arrived) ^ (held != held)
    later = jnp.stack([inverse_blocks[1], jnp.where(on_odd, swapped, kept), jnp.where(on_odd, kept, swapped)])
    later = lax.all_gather(later, FRONT, axis=0)
    near_spots, far_spots = [spots(part) for part in near_order(row_map[1, 0])]

    update = rounded(times_transposed(leaf_all, update_blocks[0])).reshape(width, PAD, rows)
    update = lax.all_to_all(jnp.concatenate([update, update], 0), PAIR, 0, 0, tiled=True)
    update = times_transposed(lanes(update), spots(pair_map))
    node_r = term_node.astype(jnp.float32) - jnp.where(odd, update, 0.0)

    first = rounded(node_r)
    update = times_transposed(rounded(times_transposed(first, node_near)), near_spots)
    update = update + times_transposed(rounded(times_transposed(first, node_far)), far_spots)
    update = rounded(update)
    at_station = receivers[0][:, None] == jnp.arange(whole)[None, :]
    station_weight = jnp.sum(jnp.where(at_station, weights[0][:, None], 0.0), axis=0)

    got = {}

    def slot(blocks, k):
        matrix = blocks[:, k + 1].reshape(whole, whole)
        places = pair_map[k * whole : (k + 1) * whole]
        places = (places[:, None] == jnp.arange(whole)[None, :]).astype(jnp.bfloat16)
        return rounded(
            lax.dot_general(
                jnp.where(odd, places, matrix), matrix, CONTRACT_FIRST, preferred_element_type=jnp.float32
            )
        )

    def beside_up(height, token):
        if height == 2:
            near, far, token = lax.optimization_barrier((node_near, node_far, token))
            got["up"] = rounded(times(near_spots, near) + times(far_spots, far))
            return ["up"]
        if height == levels:
            blocks = after(later, token)[:, 0]
            got["inverse"] = rounded(
                lax.dot_general(
                    blocks, blocks, (((0, 1), (0, 1)), ((), ())), preferred_element_type=jnp.float32
                )
            )
            return ["inverse"]
        return []

    def beside_down(height, token):
        names = []
        if height == levels:
            blocks = after(later, token)
            got["leaf"] = [slot(blocks, 0), slot(blocks, 1)]
            send_first_leaf_t(token)
            names.append("leaf")
        if height == levels - 1:
            names.append("leaf_t")
        return names

    def joined(names, *values):
        *values, extra = lax.optimization_barrier(values + ([got[n] for n in names],))
        got.update(zip(names, extra))
        return values

    def forward(update, node_r, beside):
        for height in range(2, levels + 1):
            left, right = links(height, groups)
            from_right, from_left = send(update, right), send(update, left)
            from_left, from_right = joined(beside(height, update), from_left, from_right)
            node_r = node_r - from_left.astype(jnp.float32) - from_right.astype(jnp.float32)
            if height < levels:
                update = rounded(times_transposed(rounded(node_r), got["up"]))
        return rounded(node_r)

    def backward(node_t, beside):
        node_x = rounded(node_t)
        for height in range(levels, 1, -1):
            left, right = links(height, groups)
            from_left, from_right = send(node_x, reverse(left)), send(node_x, reverse(right))
            from_left, from_right = joined(beside(height, node_x), from_left, from_right)
            new_x = rounded(node_t - times(from_left + from_right, got["up"]))
            is_child = (group & -group) == 1 << (height - 2)
            node_x = jnp.where(is_child, new_x, node_x)
        return node_x

    def leaf_step(vectors):
        return jnp.concatenate(
            [times(v, m) for v, m in zip(vectors, got["leaf"])], 1
        )

    def halves(vectors):
        return vectors[:, :whole], vectors[:, whole:]

    def through_inverse(vectors):
        return times(vectors, got["inverse"])

    carried = jnp.concatenate([station_weight, station_weight])[None, :]

    def send_first_leaf_t(token):
        leaf_t = leaf_step(halves(after(leaf_pair, token)))
        leaf_t = jnp.where(jnp.arange(PAD)[:, None] == PAD - 1, carried, leaf_t)
        got["leaf_t"] = send(leaf_t, pair_up)

    node_r = forward(update, node_r, beside_up)
    node_x = backward(through_inverse(node_r), beside_down)
    leaf_t = got["leaf_t"]
    pair_weight = jnp.concatenate([leaf_t[PAD - 1, :whole], station_weight])

    delta = rounded(leaf_t - leaf_step((node_x, node_x)))
    injected = rounded(delta.astype(jnp.float32) * pair_weight[None, :])
    update = sum(times_transposed(v, m) for v, m in zip(halves(injected), got["leaf"]))
    node_r = -jnp.where(odd, update, 0.0)
    update = rounded(times_transposed(rounded(node_r), got["up"]))

    def beside_second(height, token):
        if height == 3:
            back = after(jnp.concatenate([injected, delta[:, :whole]], 1), token)
            got["back"] = send(back, reverse(pair_up))
        if height == min(5, levels):
            back = after(got["back"], token)
            got["leaf_t"] = send(leaf_step(halves(back[:, : 2 * whole])), pair_up)
            delta_own = jnp.where(odd, delta[:, whole:], back[:, 2 * whole :])
            got["station"] = times_transposed(delta_own, at_station.astype(jnp.bfloat16))
        return []

    node_r = forward(update, node_r, beside_second)
    station, leaf_t = got["station"], got["leaf_t"]
    node_x = backward(through_inverse(node_r), lambda height, token: [])
    adjoint = rounded(leaf_t - leaf_step((node_x, node_x)))
    curve_leaf = jnp.sum(leaf_pair[:share].astype(jnp.float32) * adjoint[:share].astype(jnp.float32), axis=0)
    curve_node = jnp.sum(field_node.astype(jnp.float32) * node_x.astype(jnp.float32), axis=0)

    out = jnp.concatenate(
        [
            curve_leaf.reshape(2 * width, 1, rows),
            jnp.tile(curve_node.reshape(width, 1, rows), (2, 1, 1)),
            jnp.broadcast_to(station[None, :share], (2 * width, share, rows)),
        ],
        axis=1,
    )
    out = lax.all_to_all(out, PAIR, 0, 0, tiled=True)
    curve_leaf = jnp.sum(out[width:, 0], axis=0)
    out = jnp.where(odd, out[width:], out[:width])
    curvature = jnp.stack([curve_leaf, jnp.sum(out[:, 1], axis=0)])
    data_change = out[:, 2:].reshape(sources, rows).astype(jnp.bfloat16)
    return data_change, curvature


def solution(mesh):
    groups, width = mesh.devices.shape
    every = ("pair",) + PAIR
    split = Mesh(mesh.devices.reshape(groups // 2, 2, width // 2, 2), every)
    in_specs = (
        P(None, None, every),
        P(None, every),
        P(None, every, None),
        P(None, every, None),
        P(None, LEAF, None),
        P(LEAF, None),
        P(LEAF, None),
    )
    out_specs = (P(None, LEAF), P(None, every))
    return jax.shard_map(
        per_device, mesh=split, in_specs=in_specs, out_specs=out_specs, check_vma=False
    )
```

```python
import jax
import jax.numpy as jnp
from jax import lax
from jax.sharding import Mesh, PartitionSpec as P

LEAF = ("pair", "side")
FRONT = ("y", "core")
PAIR = ("side",) + FRONT
CONTRACT_LAST = (((1,), (1,)), ((), ()))
CONTRACT_FIRST = (((0,), (0,)), ((), ()))
PAD = 8


def times_transposed(vectors, matrix):
    return lax.dot_general(vectors, matrix, CONTRACT_LAST, preferred_element_type=jnp.float32)


def times(vectors, matrix):
    return jnp.dot(vectors, matrix, preferred_element_type=jnp.float32)


def rounded(values):
    return values.astype(jnp.bfloat16)


def after(value, *earlier):
    return lax.optimization_barrier((value,) + earlier)[0]


def links(height, groups):
    owners = [g for g in range(1, groups) if (g & -g) == 1 << (height - 1)]
    offset = 2 ** (height - 2)
    return [(g - offset, g) for g in owners], [(g + offset, g) for g in owners]


def reverse(pairs):
    return [(b, a) for a, b in pairs]


def send(value, pairs):
    return lax.ppermute(value, LEAF, pairs)


def y_blocks(block):
    count = lax.axis_size("y")

    def shifted(by):
        return lax.ppermute(block, "y", [(k, (k + by) % count) for k in range(count)])

    return [shifted(1), block, shifted(-1), shifted(2)]


def stacked(blocks):
    return jnp.concatenate(blocks, -2)


def core_swap(value):
    return lax.ppermute(value, "core", [(0, 1), (1, 0)])


def near_order(columns):
    count = lax.axis_size("y")
    blocks = columns.reshape(count, 2, -1)
    blocks = jnp.concatenate([blocks, blocks], 0)
    start = (lax.axis_index("y") + count - 1) % count
    blocks = lax.dynamic_slice_in_dim(blocks, start, count, 0)
    first, second = blocks[:, 0].reshape(-1), blocks[:, 1].reshape(-1)
    on_first = lax.axis_index("core") == 0
    return jnp.where(on_first, first, second), jnp.where(on_first, second, first)


def per_device(fields, direction, inverse_blocks, update_blocks, row_map, receivers, weights):
    groups = lax.axis_size(LEAF)
    width = lax.axis_size(FRONT)
    levels = groups.bit_length() - 1
    group = lax.axis_index(LEAF)
    odd = lax.axis_index("side") == 1
    sources, rows = fields.shape[1], fields.shape[2]
    share = sources // width
    whole = rows * width
    pair_up = [(g, g + 1) for g in range(0, groups, 2)]

    def lanes(blocks):
        blocks = blocks.reshape((-1,) + blocks.shape[-2:])
        return blocks.transpose(1, 0, 2).reshape(blocks.shape[1], -1)

    def padded(values):
        return jnp.pad(values.reshape(width, share, rows), ((0, 0), (0, PAD - share), (0, 0)))

    terms = rounded(direction[:, None, :] * fields.astype(jnp.float32))
    leaf_terms = padded(terms[0])
    map_rows = lax.dynamic_slice_in_dim(row_map[0, 0], lax.axis_index(FRONT) * rows, rows)
    digits = jnp.stack([map_rows // 32, map_rows % 32]).astype(jnp.bfloat16)
    digits = jnp.broadcast_to(digits[None], (width, 2, rows))

    def marked(values):
        return jnp.concatenate([values.reshape(width, share, rows), digits], 1)

    own = jnp.broadcast_to(leaf_terms.reshape(1, width * PAD, rows), (width, width * PAD, rows))
    own = jnp.concatenate([padded(fields[1]), padded(terms[1]), own], 1)
    message = jnp.concatenate(
        [jnp.concatenate([marked(terms[0]), own], 1), jnp.concatenate([marked(fields[0]), own], 1)], 0
    )
    node_block = update_blocks[1]
    swapped = after(jnp.where(odd, inverse_blocks[0], update_blocks[0]), message)
    message = lax.all_to_all(message, PAIR, 0, 0, tiled=True)
    message = message.reshape((2, width) + message.shape[1:])
    leaf_pair = lanes(message[:, :, :PAD])
    pair_map = leaf_pair[share].astype(jnp.float32) * 32 + leaf_pair[share + 1].astype(jnp.float32)
    pair_map = pair_map.astype(jnp.int32)
    mine = jnp.where(odd, message[1], message[0])
    field_node = lanes(mine[:, PAD : 2 * PAD])
    term_node = lanes(mine[:, 2 * PAD : 3 * PAD])
    leaf_all = lanes(mine[:, 3 * PAD :])

    def spots(columns):
        return (jnp.arange(whole)[:, None] == columns[None, :]).astype(jnp.bfloat16)

    node_near = stacked(y_blocks(node_block))
    node_far = core_swap(node_near)
    kept = jnp.where(odd, update_blocks[0], inverse_blocks[0])
    swapped = send(swapped, pair_up + reverse(pair_up))
    arrived = message[0, 0, 0, 0]
    held = node_near[0, 0] + node_near[2 * rows, 0] + node_near[3 * rows, 0]
    on_odd = odd ^ (arrived != arrived) ^ (held != held)
    later = jnp.stack([inverse_blocks[1], jnp.where(on_odd, swapped, kept), jnp.where(on_odd, kept, swapped)])
    later = lax.all_gather(later, FRONT, axis=0)
    near_spots, far_spots = [spots(part) for part in near_order(row_map[1, 0])]

    update = rounded(times_transposed(leaf_all, update_blocks[0])).reshape(width, PAD, rows)
    update = lax.all_to_all(jnp.concatenate([update, update], 0), PAIR, 0, 0, tiled=True)
    update = times_transposed(lanes(update), spots(pair_map))
    node_r = term_node.astype(jnp.float32) - jnp.where(odd, update, 0.0)

    first = rounded(node_r)
    update = times_transposed(rounded(times_transposed(first, node_near)), near_spots)
    update = update + times_transposed(rounded(times_transposed(first, node_far)), far_spots)
    update = rounded(update)
    at_station = receivers[0][:, None] == jnp.arange(whole)[None, :]
    station_weight = jnp.sum(jnp.where(at_station, weights[0][:, None], 0.0), axis=0)

    got = {}

    def slot(blocks, k):
        matrix = blocks[:, k + 1].reshape(whole, whole)
        places = pair_map[k * whole : (k + 1) * whole]
        places = (places[:, None] == jnp.arange(whole)[None, :]).astype(jnp.bfloat16)
        return rounded(
            lax.dot_general(
                jnp.where(odd, places, matrix), matrix, CONTRACT_FIRST, preferred_element_type=jnp.float32
            )
        )

    def beside_up(height, token):
        if height == 2:
            near, far, token = lax.optimization_barrier((node_near, node_far, token))
            got["up"] = rounded(times(near_spots, near) + times(far_spots, far))
            return ["up"]
        if height == levels:
            blocks = after(later, token)[:, 0]
            got["inverse"] = rounded(
                lax.dot_general(
                    blocks, blocks, (((0, 1), (0, 1)), ((), ())), preferred_element_type=jnp.float32
                )
            )
            return ["inverse"]
        return []

    def beside_down(height, token):
        names = []
        if height == levels:
            blocks = after(later, token)
            got["leaf"] = [slot(blocks, 0), slot(blocks, 1)]
            got["both"] = jnp.concatenate(got["leaf"], 1)
            send_first_leaf_t(token)
            names.append("leaf")
        if height == levels - 1:
            names.append("leaf_t")
        return names

    def joined(names, *values):
        *values, extra = lax.optimization_barrier(values + ([got[n] for n in names],))
        got.update(zip(names, extra))
        return values

    def forward(update, node_r, beside):
        for height in range(2, levels + 1):
            left, right = links(height, groups)
            if height == 3:
                from_left, from_right = send(update, left), send(update, right)
            else:
                from_right, from_left = send(update, right), send(update, left)
            from_left, from_right = joined(beside(height, update), from_left, from_right)
            node_r = node_r - from_left.astype(jnp.float32) - from_right.astype(jnp.float32)
            if height < levels:
                update = rounded(times_transposed(rounded(node_r), got["up"]))
        return rounded(node_r)

    def backward(node_t, beside):
        node_x = rounded(node_t)
        for height in range(levels, 1, -1):
            left, right = links(height, groups)
            from_left, from_right = send(node_x, reverse(left)), send(node_x, reverse(right))
            from_left, from_right = joined(beside(height, node_x), from_left, from_right)
            new_x = rounded(node_t - times(from_left + from_right, got["up"]))
            is_child = (group & -group) == 1 << (height - 2)
            node_x = jnp.where(is_child, new_x, node_x)
        return node_x

    def leaf_step(vectors):
        return jnp.concatenate(
            [times(v, m) for v, m in zip(vectors, got["leaf"])], 1
        )

    def halves(vectors):
        return vectors[:, :whole], vectors[:, whole:]

    def through_inverse(vectors):
        return times(vectors, got["inverse"])

    carried = jnp.concatenate([station_weight, station_weight])[None, :]

    def send_first_leaf_t(token):
        leaf_t = leaf_step(halves(after(leaf_pair, token)))
        leaf_t = jnp.where(jnp.arange(PAD)[:, None] == PAD - 1, carried, leaf_t)
        got["leaf_t"] = send(leaf_t, pair_up)

    node_r = forward(update, node_r, beside_up)
    node_x = backward(through_inverse(node_r), beside_down)
    leaf_t = got["leaf_t"]
    pair_weight = jnp.concatenate([leaf_t[PAD - 1, :whole], station_weight])

    delta = rounded(leaf_t - times(node_x, got["both"]))
    injected = rounded(delta.astype(jnp.float32) * pair_weight[None, :])
    update = times_transposed(injected, got["both"])
    node_r = -jnp.where(odd, update, 0.0)
    update = rounded(times_transposed(rounded(node_r), got["up"]))

    def beside_second(height, token):
        if height == 3:
            back = after(jnp.concatenate([injected, delta[:, :whole]], 1), token)
            got["back"] = send(back, reverse(pair_up))
        if height == min(5, levels):
            back = after(got["back"], token)
            got["leaf_t"] = send(leaf_step(halves(back[:, : 2 * whole])), pair_up)
            delta_own = jnp.where(odd, delta[:, whole:], back[:, 2 * whole :])
            got["station"] = times_transposed(delta_own, at_station.astype(jnp.bfloat16))
        return []

    node_r = forward(update, node_r, beside_second)
    station, leaf_t = got["station"], got["leaf_t"]
    node_x = backward(through_inverse(node_r), lambda height, token: [])
    adjoint = rounded(leaf_t - times(node_x, got["both"]))
    curve_leaf = jnp.sum(leaf_pair[:share].astype(jnp.float32) * adjoint[:share].astype(jnp.float32), axis=0)
    curve_node = jnp.sum(field_node.astype(jnp.float32) * node_x.astype(jnp.float32), axis=0)

    out = jnp.concatenate(
        [
            curve_leaf.reshape(2 * width, 1, rows),
            jnp.tile(curve_node.reshape(width, 1, rows), (2, 1, 1)),
            jnp.broadcast_to(station[None, :share], (2 * width, share, rows)),
        ],
        axis=1,
    )
    out = lax.all_to_all(out, PAIR, 0, 0, tiled=True)
    curve_leaf = jnp.sum(out[width:, 0], axis=0)
    out = jnp.where(odd, out[width:], out[:width])
    curvature = jnp.stack([curve_leaf, jnp.sum(out[:, 1], axis=0)])
    data_change = out[:, 2:].reshape(sources, rows).astype(jnp.bfloat16)
    return data_change, curvature


def solution(mesh):
    groups, width = mesh.devices.shape
    every = ("pair",) + PAIR
    split = Mesh(mesh.devices.reshape(groups // 2, 2, width // 2, 2), every)
    in_specs = (
        P(None, None, every),
        P(None, every),
        P(None, every, None),
        P(None, every, None),
        P(None, LEAF, None),
        P(LEAF, None),
        P(LEAF, None),
    )
    out_specs = (P(None, LEAF), P(None, every))
    return jax.shard_map(
        per_device, mesh=split, in_specs=in_specs, out_specs=out_specs, check_vma=False
    )
```

```python
import jax
import jax.numpy as jnp
from jax import lax
from jax.sharding import Mesh, PartitionSpec as P

LEAF = ("pair", "side")
FRONT = ("y", "core")
PAIR = ("side",) + FRONT
CONTRACT_LAST = (((1,), (1,)), ((), ()))
CONTRACT_FIRST = (((0,), (0,)), ((), ()))
PAD = 8


def times_transposed(vectors, matrix):
    return lax.dot_general(vectors, matrix, CONTRACT_LAST, preferred_element_type=jnp.float32)


def times(vectors, matrix):
    return jnp.dot(vectors, matrix, preferred_element_type=jnp.float32)


def rounded(values):
    return values.astype(jnp.bfloat16)


def after(value, *earlier):
    return lax.optimization_barrier((value,) + earlier)[0]


def links(height, groups):
    owners = [g for g in range(1, groups) if (g & -g) == 1 << (height - 1)]
    offset = 2 ** (height - 2)
    return [(g - offset, g) for g in owners], [(g + offset, g) for g in owners]


def reverse(pairs):
    return [(b, a) for a, b in pairs]


def send(value, pairs):
    return lax.ppermute(value, LEAF, pairs)


def y_blocks(block):
    count = lax.axis_size("y")

    def shifted(by):
        return lax.ppermute(block, "y", [(k, (k + by) % count) for k in range(count)])

    return [shifted(1), block, shifted(-1), shifted(2)]


def stacked(blocks):
    return jnp.concatenate(blocks, -2)


def core_swap(value):
    return lax.ppermute(value, "core", [(0, 1), (1, 0)])


def near_order(columns):
    count = lax.axis_size("y")
    blocks = columns.reshape(count, 2, -1)
    blocks = jnp.concatenate([blocks, blocks], 0)
    start = (lax.axis_index("y") + count - 1) % count
    blocks = lax.dynamic_slice_in_dim(blocks, start, count, 0)
    first, second = blocks[:, 0].reshape(-1), blocks[:, 1].reshape(-1)
    on_first = lax.axis_index("core") == 0
    return jnp.where(on_first, first, second), jnp.where(on_first, second, first)


def per_device(fields, direction, inverse_blocks, update_blocks, row_map, receivers, weights):
    groups = lax.axis_size(LEAF)
    width = lax.axis_size(FRONT)
    levels = groups.bit_length() - 1
    group = lax.axis_index(LEAF)
    odd = lax.axis_index("side") == 1
    sources, rows = fields.shape[1], fields.shape[2]
    share = sources // width
    whole = rows * width
    pair_up = [(g, g + 1) for g in range(0, groups, 2)]

    def lanes(blocks):
        blocks = blocks.reshape((-1,) + blocks.shape[-2:])
        return blocks.transpose(1, 0, 2).reshape(blocks.shape[1], -1)

    def padded(values):
        return jnp.pad(values.reshape(width, share, rows), ((0, 0), (0, PAD - share), (0, 0)))

    terms = rounded(direction[:, None, :] * fields.astype(jnp.float32))
    leaf_terms = padded(terms[0])
    own = jnp.broadcast_to(leaf_terms.reshape(1, width * PAD, rows), (width, width * PAD, rows))
    own = jnp.concatenate([padded(fields[1]), padded(terms[1]), own], 1)
    message = jnp.concatenate(
        [jnp.concatenate([leaf_terms, own], 1), jnp.concatenate([padded(fields[0]), own], 1)], 0
    )
    node_block = update_blocks[1]
    swapped = after(jnp.where(odd, inverse_blocks[0], update_blocks[0]), message)
    message = lax.all_to_all(message, PAIR, 0, 0, tiled=True)
    message = message.reshape((2, width) + message.shape[1:])
    leaf_pair = lanes(message[:, :, :PAD])
    mine = jnp.where(odd, message[1], message[0])
    field_node = lanes(mine[:, PAD : 2 * PAD])
    term_node = lanes(mine[:, 2 * PAD : 3 * PAD])
    leaf_all = lanes(mine[:, 3 * PAD :])

    def spots(columns):
        return (jnp.arange(whole)[:, None] == columns[None, :]).astype(jnp.bfloat16)

    node_near = stacked(y_blocks(node_block))
    node_far = core_swap(node_near)
    kept = jnp.where(odd, update_blocks[0], inverse_blocks[0])
    swapped = send(swapped, pair_up + reverse(pair_up))
    arrived = message[0, 0, 0, 0]
    held = node_near[0, 0] + node_near[2 * rows, 0] + node_near[3 * rows, 0]
    on_odd = odd ^ (arrived != arrived) ^ (held != held)
    later = jnp.stack([inverse_blocks[1], jnp.where(on_odd, swapped, kept), jnp.where(on_odd, kept, swapped)])
    later = lax.all_gather(later, FRONT, axis=0)
    near_spots, far_spots = [spots(part) for part in near_order(row_map[1, 0])]

    map_rows = lax.dynamic_slice_in_dim(row_map[0, 0], lax.axis_index(FRONT) * rows, rows)
    digits = jnp.stack([map_rows // 32, map_rows % 32]).astype(jnp.bfloat16)
    digits = jnp.broadcast_to(digits[None], (width, 2, rows))
    update = rounded(times_transposed(leaf_all, update_blocks[0])).reshape(width, PAD, rows)
    update = jnp.concatenate([update[:, :share], digits], 1)
    update = lax.all_to_all(jnp.concatenate([update, update], 0), PAIR, 0, 0, tiled=True)
    update = lanes(update)
    pair_map = update[share].astype(jnp.float32) * 32 + update[share + 1].astype(jnp.float32)
    pair_map = pair_map.astype(jnp.int32)
    update = times_transposed(update, spots(pair_map))
    node_r = term_node.astype(jnp.float32) - jnp.where(odd, update, 0.0)

    node_up = rounded(times(near_spots, node_near) + times(far_spots, node_far))
    update = rounded(times_transposed(rounded(node_r), node_up))

    at_station = receivers[0][:, None] == jnp.arange(whole)[None, :]
    station_weight = jnp.sum(jnp.where(at_station, weights[0][:, None], 0.0), axis=0)

    got = {"up": node_up}

    def slot(blocks, k):
        matrix = blocks[:, k + 1].reshape(whole, whole)
        places = pair_map[k * whole : (k + 1) * whole]
        places = (places[:, None] == jnp.arange(whole)[None, :]).astype(jnp.bfloat16)
        return rounded(
            lax.dot_general(
                jnp.where(odd, places, matrix), matrix, CONTRACT_FIRST, preferred_element_type=jnp.float32
            )
        )

    def beside_up(height, token):
        if height == levels:
            got["factor"] = later[:, 0]
            return []
        return []

    def beside_down(height, token):
        names = []
        if height == levels - 1:
            blocks = got["factor"]
            got["inverse"] = rounded(
                lax.dot_general(
                    blocks, blocks, (((0, 1), (0, 1)), ((), ())), preferred_element_type=jnp.float32
                )
            )
            names.append("inverse")
        if height == levels:
            blocks = after(later, token)
            got["leaf"] = [slot(blocks, 0), slot(blocks, 1)]
            send_first_leaf_t(token)
            names.append("leaf")
        if height == levels - 1:
            names.append("leaf_t")
        return names

    def joined(names, *values):
        *values, extra = lax.optimization_barrier(values + ([got[n] for n in names],))
        got.update(zip(names, extra))
        return values

    def forward(update, node_r, beside):
        for height in range(2, levels + 1):
            left, right = links(height, groups)
            if height == 3:
                from_left, from_right = send(update, left), send(update, right)
            else:
                from_right, from_left = send(update, right), send(update, left)
            from_left, from_right = joined(beside(height, update), from_left, from_right)
            node_r = node_r - from_left.astype(jnp.float32) - from_right.astype(jnp.float32)
            if height < levels:
                update = rounded(times_transposed(rounded(node_r), got["up"]))
        return rounded(node_r)

    def backward(node_t, beside):
        node_x = rounded(node_t)
        for height in range(levels, 1, -1):
            left, right = links(height, groups)
            from_left, from_right = send(node_x, reverse(left)), send(node_x, reverse(right))
            from_left, from_right = joined(beside(height, node_x), from_left, from_right)
            new_x = rounded(node_t - times(from_left + from_right, got["up"]))
            is_child = (group & -group) == 1 << (height - 2)
            node_x = jnp.where(is_child, new_x, node_x)
        return node_x

    def leaf_step(vectors):
        return jnp.concatenate(
            [times(v, m) for v, m in zip(vectors, got["leaf"])], 1
        )

    def halves(vectors):
        return vectors[:, :whole], vectors[:, whole:]

    def through_inverse(vectors):
        if "inverse" in got:
            return times(vectors, got["inverse"])
        blocks = got["factor"]
        solved = lax.dot_general(
            vectors, blocks, (((1,), (2,)), ((), ())), preferred_element_type=jnp.float32
        )
        return lax.dot_general(
            rounded(solved), blocks, (((1, 2), (0, 1)), ((), ())), preferred_element_type=jnp.float32
        )

    carried = jnp.concatenate([station_weight, station_weight])[None, :]

    def send_first_leaf_t(token):
        leaf_t = leaf_step(halves(after(leaf_pair, token)))
        leaf_t = jnp.where(jnp.arange(PAD)[:, None] == PAD - 1, carried, leaf_t)
        got["leaf_t"] = send(leaf_t, pair_up)

    node_r = forward(update, node_r, beside_up)
    node_x = backward(through_inverse(node_r), beside_down)
    leaf_t = got["leaf_t"]
    pair_weight = jnp.concatenate([leaf_t[PAD - 1, :whole], station_weight])

    delta = rounded(leaf_t - leaf_step((node_x, node_x)))
    injected = rounded(delta.astype(jnp.float32) * pair_weight[None, :])
    update = sum(times_transposed(v, m) for v, m in zip(halves(injected), got["leaf"]))
    node_r = -jnp.where(odd, update, 0.0)
    update = rounded(times_transposed(rounded(node_r), got["up"]))

    def beside_second(height, token):
        if height == 3:
            back = after(jnp.concatenate([injected, delta[:, :whole]], 1), token)
            got["back"] = send(back, reverse(pair_up))
        if height == min(5, levels):
            back = after(got["back"], token)
            got["leaf_t"] = send(leaf_step(halves(back[:, : 2 * whole])), pair_up)
            delta_own = jnp.where(odd, delta[:, whole:], back[:, 2 * whole :])
            got["station"] = times_transposed(delta_own, at_station.astype(jnp.bfloat16))
        return []

    node_r = forward(update, node_r, beside_second)
    station, leaf_t = got["station"], got["leaf_t"]
    node_x = backward(through_inverse(node_r), lambda height, token: [])
    adjoint = rounded(leaf_t - leaf_step((node_x, node_x)))
    curve_leaf = jnp.sum(leaf_pair[:share].astype(jnp.float32) * adjoint[:share].astype(jnp.float32), axis=0)
    curve_node = jnp.sum(field_node.astype(jnp.float32) * node_x.astype(jnp.float32), axis=0)

    out = jnp.concatenate(
        [
            curve_leaf.reshape(2 * width, 1, rows),
            jnp.tile(curve_node.reshape(width, 1, rows), (2, 1, 1)),
            jnp.broadcast_to(station[None, :share], (2 * width, share, rows)),
        ],
        axis=1,
    )
    out = lax.all_to_all(out, PAIR, 0, 0, tiled=True)
    curve_leaf = jnp.sum(out[width:, 0], axis=0)
    out = jnp.where(odd, out[width:], out[:width])
    curvature = jnp.stack([curve_leaf, jnp.sum(out[:, 1], axis=0)])
    data_change = out[:, 2:].reshape(sources, rows).astype(jnp.bfloat16)
    return data_change, curvature


def solution(mesh):
    groups, width = mesh.devices.shape
    every = ("pair",) + PAIR
    split = Mesh(mesh.devices.reshape(groups // 2, 2, width // 2, 2), every)
    in_specs = (
        P(None, None, every),
        P(None, every),
        P(None, every, None),
        P(None, every, None),
        P(None, LEAF, None),
        P(LEAF, None),
        P(LEAF, None),
    )
    out_specs = (P(None, LEAF), P(None, every))
    return jax.shard_map(
        per_device, mesh=split, in_specs=in_specs, out_specs=out_specs, check_vma=False
    )
```
